128 devices in a mesh: row: 8 (over z, core), col: 16 (over y, x).
Axes of the slice: x: 4, y: 4, z: 4, core: 2. Of those that a mesh axis runs over, the one named last changes fastest.
Arguments:
- amplitudes: float32 [4096, 8192], P(('row', 'col')), may hold values from -6 to 6
- intermediates: float32 [4096, 8192], P(('row', 'col')), may hold values from -0.09375 to 0.09375
Outputs:
- sigma: float32 [8192, 8192], P('row', 'col')
The draws below stay inside these ranges and needn't reach their ends.
All inputs are finite; a program needn't handle non-finite values.
Results may differ from the reference program's by a relative error of at most 0.00007.
Values sent between devices are 32-bit elements; how exact they have to be, the bound alone decides.
No kernel may reach another device: no remote copies, remote signals or barrier semaphores. Data moves between devices by JAX's collectives and lax.ppermute only.
A program may use at most 128 MiB of HBM per device.

```python
import jax
import jax.numpy as jnp
from jax import lax

ROWS = 8192
COLS = 8192
INNER = 4096


def shard_levels(rng, extent, shards, low, high):
    gain = 1.0
    for position, blocks in shards:
        heights = jax.random.uniform(jax.random.fold_in(jax.random.fold_in(rng, 6), position), (blocks,), jnp.float32, low / len(shards), high / len(shards))
        gain = gain * jnp.repeat(jnp.exp(heights), extent[position] // blocks).reshape((-1,) + (1,) * (len(extent) - 1 - position))
    return gain


def normal_values(key, shape, scale, bound, split=(), kind=jnp.bfloat16):
    entries = scale * jax.random.normal(key, shape, jnp.float32)
    if split:
        entries = entries * shard_levels(key, shape, split, -0.22, 0.18)
    return jnp.clip(entries, -bound, bound).astype(kind)


def setup_inputs(seed: int = 0) -> dict:
    streams_of = jax.random.split(jax.random.key(seed), 3)
    return {
        "amplitudes": normal_values(streams_of[0], (INNER, ROWS), 1.0, 6.0, ((0, 128),), jnp.float32),
        "intermediates": normal_values(streams_of[1], (INNER, COLS), INNER ** -0.5, 0.09375, ((0, 128),), jnp.float32),
    }


def reference(amplitudes, intermediates):
    return lax.dot_general(amplitudes, intermediates, (((0,), (0,)), ((), ())), precision=lax.Precision.HIGHEST, preferred_element_type=jnp.float32)
```

```python
import functools

import jax
import jax.numpy as jnp
from jax import lax
from jax.experimental import pallas as pl
from jax.experimental.pallas import tpu as pltpu
from jax.sharding import Mesh, PartitionSpec as P

N = 4
ALL = ("z", "c", "y", "x")
VMEM_LIMIT = 48 * 1024 * 1024


def shift(value, axis, step):
    return lax.ppermute(value, axis, [(i, (i + step) % N) for i in range(N)])


def split(value):
    high = value.astype(jnp.bfloat16)
    low = (value - high.astype(jnp.float32)).astype(jnp.bfloat16)
    return high, low


def dot(first, second):
    return lax.dot_general(
        first, second, (((1,), (0,)), ((), ())), preferred_element_type=jnp.float32
    )


def arrange_kernel(place, b_ref, x_ref, y_ref):
    half = x_ref.shape[2] // N
    for dy in range(N):
        for dx in range(N):
            block = lax.rem(place[0] + dy, N) * N + lax.rem(place[1] + dx, N)
            first = pl.multiple_of(block * 2 * half, 2 * half)
            x_ref[dy, :, dx * half : (dx + 1) * half] = b_ref[:, pl.ds(first, half)]
            second = pl.multiple_of(first + half, half)
            y_ref[dx, :, dy * half : (dy + 1) * half] = b_ref[:, pl.ds(second, half)]


def arrange(b, place):
    rows, columns = b.shape
    out = jax.ShapeDtypeStruct((N, rows, columns // (2 * N)), b.dtype)
    return pl.pallas_call(
        arrange_kernel,
        out_shape=(out, out),
        in_specs=[
            pl.BlockSpec(memory_space=pltpu.SMEM),
            pl.BlockSpec(memory_space=pltpu.VMEM),
        ],
        out_specs=(pl.BlockSpec(memory_space=pltpu.VMEM),) * 2,
        compiler_params=pltpu.CompilerParams(vmem_limit_bytes=VMEM_LIMIT),
        name="arrange",
    )(place, b)


def product_kernel(steps, has_start, *refs):
    count = len(steps)
    a_refs, refs = refs[:count], refs[count:]
    b_ref, refs = refs[0], refs[1:]
    start_ref, refs = (refs[0], refs[1:]) if has_start else (None, refs)
    out_ref, high_ref, low_ref = refs

    @pl.when(pl.program_id(0) == 0)
    def _():
        for i in range(count):
            high_ref[i], low_ref[i] = split(a_refs[i][...])

    depth = a_refs[0].shape[1]
    total = start_ref[0] if has_start else None
    for i, step in enumerate(steps):
        block = b_ref[:, step].reshape(depth, b_ref.shape[3])
        high, low = split(block)
        term = dot(high_ref[i], high) + dot(high_ref[i], low) + dot(low_ref[i], high)
        total = term if total is None else total + term
    out_ref[0] = total


def product(blocks, steps, b, start=None):
    rows, depth = blocks[0].shape
    ranks, _, slab, columns = b.shape
    width = columns // N
    operands = list(blocks) + [b]
    in_specs = [pl.BlockSpec((rows, depth), lambda r: (0, 0)) for _ in blocks]
    in_specs.append(pl.BlockSpec((ranks, N, slab, width), lambda r: (0, 0, 0, r)))
    if start is not None:
        operands.append(start)
        in_specs.append(pl.BlockSpec((1, rows, width), lambda r: (r, 0, 0)))
    flops = 6 * rows * depth * len(blocks) * columns
    return pl.pallas_call(
        functools.partial(product_kernel, tuple(steps), start is not None),
        grid=(N,),
        out_shape=jax.ShapeDtypeStruct((N, rows, width), jnp.float32),
        in_specs=in_specs,
        out_specs=pl.BlockSpec((1, rows, width), lambda r: (r, 0, 0)),
        scratch_shapes=[pltpu.VMEM((len(blocks), rows, depth), jnp.bfloat16)] * 2,
        compiler_params=pltpu.CompilerParams(vmem_limit_bytes=VMEM_LIMIT),
        cost_estimate=pl.CostEstimate(
            flops=flops, bytes_accessed=4 * rows * columns * 2, transcendentals=0
        ),
        name="product",
    )(*operands)


def gather_a(own, axis):
    half = own.shape[0] // 2
    behind = shift(own, axis, 1)
    ahead = shift(own, axis, -1)
    top = shift(behind[:half], axis, 1)
    bottom = shift(ahead[half:], axis, -1)
    return behind, ahead, jnp.concatenate([top, bottom], 0)


def reduce_c(part, axis):
    half = part.shape[1] // 2
    top = shift(part[2, :half], axis, 1)
    bottom = shift(part[2, half:], axis, -1)
    forward = jnp.concatenate([part[1, :half] + top, part[1, half:]], 0)
    backward = jnp.concatenate([part[3, :half], part[3, half:] + bottom], 0)
    return part[0] + (shift(forward, axis, 1) + shift(backward, axis, -1))


def scatter_b(blocks, axis):
    return [blocks[0]] + [shift(blocks[d], axis, d) for d in range(1, N)]


def gather_b(blocks):
    block = jnp.stack(blocks, 0)
    return lax.all_gather(block, ("z", "c"), axis=0, tiled=False)


def shards(a, b):
    place = jnp.stack([lax.axis_index("y"), lax.axis_index("x")]).astype(jnp.int32)
    bx, by = arrange(b, place)
    bx = scatter_b(bx, "y")
    by = scatter_b(by, "x")
    az = lax.all_to_all(a, ("z", "c"), split_axis=1, concat_axis=0, tiled=True)
    own = az.T
    panel_x = gather_b(bx)
    panel_y = gather_b(by)
    outs = []
    for axis, along, panel in (("y", "x", panel_x), ("x", "y", panel_y)):
        behind, ahead, far = gather_a(own, axis)
        part = product([own, behind, ahead], (0, 1, 3), panel)
        part = product([far], (2,), panel, part)
        outs.append(reduce_c(part, along))
    return jnp.concatenate(outs, 1)


def solution(mesh):
    fine = Mesh(mesh.devices.reshape(N, 2, N, N), ALL)
    return jax.shard_map(
        shards,
        mesh=fine,
        in_specs=(P(ALL, None), P(ALL, None)),
        out_specs=P(("z", "c"), ("y", "x")),
        check_vma=False,
    )
```

```python
import functools
import itertools

import jax
import jax.numpy as jnp
from jax import lax
from jax.experimental import pallas as pl
from jax.experimental.pallas import tpu as pltpu
from jax.sharding import Mesh, PartitionSpec as P

N = 4
ALL = ("z", "c", "y", "x")
VMEM_LIMIT = 16 * 1024 * 1024


def permute(value, target):
    pairs = []
    for z, c, y, x in itertools.product(range(N), range(2), range(N), range(N)):
        tz, tc, ty, tx = target(z, c, y, x)
        place = ((tz % N * 2 + tc % 2) * N + ty % N) * N + tx % N
        pairs.append((((z * 2 + c) * N + y) * N + x, place))
    return lax.ppermute(value, ALL, pairs)


def swap(value):
    return permute(value, lambda z, c, y, x: (z, 1 - c, y, x))


def along_z(value, step):
    return permute(value, lambda z, c, y, x: (z + step * (1 - 2 * c), c, y, x))


def along_gather(value, step):
    return permute(value, lambda z, c, y, x: (z, c, y + step * (1 - c), x + step * c))


def along_reduce(value, step):
    return permute(value, lambda z, c, y, x: (z, c, y + step * c, x + step * (1 - c)))


def split(value):
    high = value.astype(jnp.bfloat16)
    low = (value - high.astype(jnp.float32)).astype(jnp.bfloat16)
    return high, low


def dot(first, second):
    return lax.dot_general(
        first, second, (((1,), (0,)), ((), ())), preferred_element_type=jnp.float32
    )


SMEM = pl.BlockSpec(memory_space=pltpu.SMEM)
VMEM = pl.BlockSpec(memory_space=pltpu.VMEM)
ANY = pl.BlockSpec(memory_space=pl.ANY)
HBM = pl.BlockSpec(memory_space=pltpu.HBM)
PARAMS = pltpu.CompilerParams(vmem_limit_bytes=VMEM_LIMIT)


def prepare_a_kernel(place, a_ref, own_ref, two_ref, side_ref, pass_ref):
    z, c = place[0], place[1]
    wide = own_ref.shape[1]
    half = wide // 2

    def piece(step, part=0, width=wide):
        start = lax.rem(z + step, N) * wide + part * half
        return a_ref[:, pl.ds(pl.multiple_of(start, half), width)]

    own_ref[...] = piece(0)
    two_ref[...] = piece(2)
    side_ref[...] = piece(1 + 2 * c)
    for part in range(2):
        pass_ref[part] = piece(0, part, half)
        pass_ref[2 + part] = piece(3 - 2 * c, part, half)


def prepare_a(a, place):
    rows, columns = a.shape
    piece = jax.ShapeDtypeStruct((rows, columns // N), a.dtype)
    passed = jax.ShapeDtypeStruct((N, rows, columns // (2 * N)), a.dtype)
    return pl.pallas_call(
        prepare_a_kernel,
        out_shape=(piece, piece, piece, passed),
        in_specs=[SMEM, VMEM],
        out_specs=(VMEM,) * 4,
        compiler_params=PARAMS,
        name="prepare_a",
    )(place, a)


def prepare_b_kernel(place, b_ref, keep_ref, pass_ref):
    c, y, x = place[1], place[2], place[3]
    width = keep_ref.shape[2] // N
    for core, ref in ((c, keep_ref), (1 - c, pass_ref)):
        for g in range(N):
            for h in range(N):
                ty = lax.rem(y + g * (1 - core) + h * core, N)
                tx = lax.rem(x + g * core + h * (1 - core), N)
                start = pl.multiple_of(((ty * N + tx) * 2 + core) * width, width)
                ref[g, :, h * width : (h + 1) * width] = b_ref[:, pl.ds(start, width)]


def prepare_b(b, place):
    rows, columns = b.shape
    part = jax.ShapeDtypeStruct((N, rows, columns // (2 * N)), b.dtype)
    return pl.pallas_call(
        prepare_b_kernel,
        out_shape=(part, part),
        in_specs=[SMEM, VMEM],
        out_specs=(VMEM, VMEM),
        compiler_params=PARAMS,
        name="prepare_b",
    )(place, b)


def join_a_kernel(side, got, out_ref):
    rows, wide = side.shape
    half = wide // 2
    out_ref[:rows] = side[...]
    for part in range(2):
        out_ref[rows:, part * half : (part + 1) * half] = got[2 + part]


def join_a(side, got):
    rows, wide = side.shape
    return pl.pallas_call(
        join_a_kernel,
        out_shape=jax.ShapeDtypeStruct((2 * rows, wide), side.dtype),
        in_specs=[VMEM] * 2,
        out_specs=VMEM,
        compiler_params=PARAMS,
        name="join_a",
    )(side, got)


def join_b_kernel(keep, got, *refs):
    rows = keep.shape[1]
    for g in range(N):
        refs[g][:rows] = keep[g]
        refs[g][rows:] = got[g]


def join_b(keep, got):
    _, rows, columns = keep.shape
    return pl.pallas_call(
        join_b_kernel,
        out_shape=(jax.ShapeDtypeStruct((2 * rows, columns), keep.dtype),) * N,
        in_specs=[VMEM] * 2,
        out_specs=(VMEM,) * N,
        compiler_params=PARAMS,
        name="join_b",
    )(keep, got)


def turn_kernel(place, own, got, side, two, two_got, side_got, *refs):
    out_ref = refs[-1]
    half = out_ref.shape[1]
    rows = own.shape[0]
    for part in range(2):
        which = lax.rem(place[1] + part, 2)
        columns = pl.ds(pl.multiple_of(which * half, half), half)
        blocks = [
            own[:, columns],
            got[which],
            side[:, columns],
            two[:, columns],
            two_got[:, columns],
            side_got[rows:, columns],
            side_got[:rows, columns],
        ]
        out_ref[part] = jnp.concatenate(blocks, 0).T


def turn(place, parts, after):
    rows, columns = parts[0].shape
    return pl.pallas_call(
        turn_kernel,
        out_shape=jax.ShapeDtypeStruct((2, columns // 2, 2 * N * rows), jnp.float32),
        in_specs=[SMEM] + [VMEM] * 6 + [ANY] * len(after),
        out_specs=VMEM,
        compiler_params=PARAMS,
        name="turn",
    )(place, *parts, *after)


GATHERED = (0, 1, 3)


def split_a_kernel(a0, a1, a3, high_ref, low_ref):
    depth = a0.shape[2]
    for half in range(2):
        for i, ref in enumerate((a0, a1, a3)):
            place = slice(i * depth, (i + 1) * depth)
            high_ref[half, :, place], low_ref[half, :, place] = split(ref[half])


def split_a(blocks):
    _, rows, depth = blocks[0].shape
    out = jax.ShapeDtypeStruct((2, rows, 3 * depth), jnp.bfloat16)
    return pl.pallas_call(
        split_a_kernel,
        out_shape=(out, out),
        in_specs=[VMEM] * 3,
        out_specs=(VMEM, VMEM),
        compiler_params=PARAMS,
        name="split_a",
    )(*blocks)


def split_b_kernel(*refs):
    high_ref, low_ref = refs[N:]
    slab = refs[0].shape[1]
    for i, g in enumerate(GATHERED + (2,)):
        for s in range(N):
            place = slice((i * N + s) * slab, (i * N + s + 1) * slab)
            high_ref[place], low_ref[place] = split(refs[s][g])


def split_b(panels):
    _, slab, columns = panels[0].shape
    out = jax.ShapeDtypeStruct((N * N * slab, columns), jnp.bfloat16)
    return pl.pallas_call(
        split_b_kernel,
        out_shape=(out, out),
        in_specs=[VMEM] * N,
        out_specs=(VMEM, VMEM),
        compiler_params=PARAMS,
        name="split_b",
    )(*panels)


TILE = 512


def one_product(half, r, high, low, far_high, far_low, bh, bl, out_ref):
    near = high.shape[2]
    rows, width = out_ref.shape
    columns = slice(r * width, (r + 1) * width)
    for start in range(0, rows, TILE):
        tile = slice(start, start + TILE)
        total = dot(high[half, tile], bh[:near, columns])
        total += dot(high[half, tile], bl[:near, columns])
        total += dot(low[half, tile], bh[:near, columns])
        total += dot(far_high[half, tile], bh[near:, columns])
        total += dot(far_high[half, tile], bl[near:, columns])
        total += dot(far_low[half, tile], bh[near:, columns])
        out_ref[tile] = total


def first_kernel(high, low, top, bottom, bh, bl, far_high, far_low, *out_refs):
    far_high[0], far_low[0] = split(top[...])
    far_high[1], far_low[1] = split(bottom[...])
    for half, ref in enumerate(out_refs):
        one_product(half, 2, high, low, far_high, far_low, bh, bl, ref)


def product_kernel(tasks, high, low, far_high, far_low, bh, bl, *out_refs):
    for (half, r), ref in zip(tasks, out_refs):
        one_product(half, r, high, low, far_high, far_low, bh, bl, ref)


def cost(rows, depth, width, count):
    return pl.CostEstimate(
        flops=6 * rows * depth * width * count,
        bytes_accessed=4 * rows * width * count,
        transcendentals=0,
    )


def first_product(high, low, top, bottom, bh, bl):
    rows, depth = top.shape
    width = bh.shape[1] // N
    far = jax.ShapeDtypeStruct((2, rows, depth), jnp.bfloat16)
    out = jax.ShapeDtypeStruct((rows, width), jnp.float32)
    return pl.pallas_call(
        first_kernel,
        out_shape=(far, far, out, out),
        in_specs=[VMEM] * 6,
        out_specs=(VMEM,) * 4,
        compiler_params=PARAMS,
        cost_estimate=cost(rows, N * depth, width, 2),
        name="first_product",
    )(high, low, top, bottom, bh, bl)


def product(tasks, high, low, far_high, far_low, bh, bl):
    _, rows, depth = far_high.shape
    width = bh.shape[1] // N
    out = jax.ShapeDtypeStruct((rows, width), jnp.float32)
    return pl.pallas_call(
        functools.partial(product_kernel, tasks),
        out_shape=(out,) * len(tasks),
        in_specs=[VMEM] * 6,
        out_specs=(VMEM,) * len(tasks),
        compiler_params=PARAMS,
        cost_estimate=cost(rows, N * depth, width, len(tasks)),
        name="product",
    )(high, low, far_high, far_low, bh, bl)


def finish_kernel(place, top0, top3, top1, got, out_ref):
    tile, width = out_ref.shape
    rows = pl.ds(pl.multiple_of(pl.program_id(0) * tile, tile), tile)
    mine = top0[rows] + top3[rows] + top1[rows]
    theirs = got[rows]
    width //= 2

    @pl.when(place[1] == 0)
    def _():
        out_ref[:, :width] = mine
        out_ref[:, width:] = theirs

    @pl.when(place[1] == 1)
    def _():
        out_ref[:, :width] = theirs
        out_ref[:, width:] = mine


def finish(place, top0, top3, top1, got):
    rows, width = top0.shape
    tile = rows // 4
    return pl.pallas_call(
        finish_kernel,
        grid=(4,),
        out_shape=jax.ShapeDtypeStruct((rows, 2 * width), jnp.float32),
        in_specs=[SMEM] + [VMEM] * 4,
        out_specs=pl.BlockSpec((tile, 2 * width), lambda m: (m, 0)),
        compiler_params=PARAMS,
        name="finish",
    )(place, top0, top3, top1, got)


TOP, BOTTOM = 0, 1


def shards(a, b):
    place = jnp.stack([lax.axis_index(name) for name in ALL]).astype(jnp.int32)
    own, two, side, handed = prepare_a(a, place)
    two = along_z(two, 2)
    got = swap(handed)
    side = along_z(join_a(side, got), 1)
    keep, give = prepare_b(b, place)
    pieces = join_b(keep, swap(give))

    panel = [pieces[0]] + [along_gather(pieces[g], g) for g in range(1, N)]
    two, side, panel = lax.optimization_barrier((two, side, panel))
    near = turn(place, (own, got, side, two, swap(two), swap(side)), ())

    panels = [jnp.stack(panel, 0)]
    for _ in range(N - 1):
        panels.append(along_z(panels[-1], 1))

    behind = along_gather(near, 1)
    ahead = along_gather(near, -1)
    top = along_gather(behind[TOP], 1)
    bottom = along_gather(ahead[BOTTOM], -1)

    high, low = split_a((near, behind, ahead))
    bh, bl = split_b(panels)
    far_high, far_low, top2, bottom2 = first_product(high, low, top, bottom, bh, bl)
    operands = (high, low, far_high, far_low, bh, bl)
    bottom1, top3 = product(((BOTTOM, 1), (TOP, 3)), *operands)
    top1, bottom3 = product(((TOP, 1), (BOTTOM, 3)), *operands)
    top0, bottom0 = product(((TOP, 0), (BOTTOM, 0)), *operands)

    top2 = along_reduce(top2, 1)
    bottom2 = along_reduce(bottom2, -1)
    bottom1 = along_reduce(bottom1, 1)
    top3 = along_reduce(top3, -1)
    top1 = along_reduce(top1 + top2, 1)
    bottom3 = along_reduce(bottom3 + bottom2, -1)
    got = swap(bottom0 + bottom1 + bottom3)
    return finish(place, top0, top3, top1, got)


def solution(mesh):
    fine = Mesh(mesh.devices.reshape(N, 2, N, N), ALL)
    return jax.shard_map(
        shards,
        mesh=fine,
        in_specs=(P(ALL, None), P(ALL, None)),
        out_specs=P(("z", "c"), ("y", "x")),
        check_vma=False,
    )
```

```python
import functools
import itertools

import jax
import jax.numpy as jnp
from jax import lax
from jax.experimental import pallas as pl
from jax.experimental.pallas import tpu as pltpu
from jax.sharding import Mesh, PartitionSpec as P

N = 4
ALL = ("z", "c", "y", "x")
VMEM_LIMIT = 16 * 1024 * 1024


def permute(value, target):
    pairs = []
    for z, c, y, x in itertools.product(range(N), range(2), range(N), range(N)):
        tz, tc, ty, tx = target(z, c, y, x)
        place = ((tz % N * 2 + tc % 2) * N + ty % N) * N + tx % N
        pairs.append((((z * 2 + c) * N + y) * N + x, place))
    return lax.ppermute(value, ALL, pairs)


def swap(value):
    return permute(value, lambda z, c, y, x: (z, 1 - c, y, x))


def along_z(value, step):
    return permute(value, lambda z, c, y, x: (z + step * (1 - 2 * c), c, y, x))


def along_gather(value, step):
    return permute(value, lambda z, c, y, x: (z, c, y + step * (1 - c), x + step * c))


def along_reduce(value, step):
    return permute(value, lambda z, c, y, x: (z, c, y + step * c, x + step * (1 - c)))


def split(value):
    high = value.astype(jnp.bfloat16)
    low = (value - high.astype(jnp.float32)).astype(jnp.bfloat16)
    return high, low


def dot(first, second):
    return lax.dot_general(
        first, second, (((1,), (0,)), ((), ())), preferred_element_type=jnp.float32
    )


SMEM = pl.BlockSpec(memory_space=pltpu.SMEM)
VMEM = pl.BlockSpec(memory_space=pltpu.VMEM)
ANY = pl.BlockSpec(memory_space=pl.ANY)
HBM = pl.BlockSpec(memory_space=pltpu.HBM)
PARAMS = pltpu.CompilerParams(vmem_limit_bytes=VMEM_LIMIT)


def prepare_a_kernel(place, a_ref, own_ref, two_ref, side_ref, pass_ref):
    z, c = place[0], place[1]
    half = own_ref.shape[2]

    def piece(step, part):
        start = (lax.rem(z + step, N) * 2 + part) * half
        return a_ref[:, pl.ds(pl.multiple_of(start, half), half)]

    for part in range(2):
        mine = lax.rem(c + part, 2)
        own_ref[part] = piece(0, mine)
        two_ref[part] = piece(2, mine)
        side_ref[part] = piece(1 + 2 * c, mine)
        pass_ref[0, part] = piece(0, 1 - mine)
        pass_ref[1, part] = piece(3 - 2 * c, 1 - mine)


def prepare_a(a, place):
    rows, columns = a.shape
    piece = jax.ShapeDtypeStruct((2, rows, columns // (2 * N)), a.dtype)
    passed = jax.ShapeDtypeStruct((2, 2, rows, columns // (2 * N)), a.dtype)
    return pl.pallas_call(
        prepare_a_kernel,
        out_shape=(piece, piece, piece, passed),
        in_specs=[SMEM, VMEM],
        out_specs=(VMEM,) * 4,
        compiler_params=PARAMS,
        name="prepare_a",
    )(place, a)


STREAMS = 2
ORDER = (2, 1, 3, 0)


def prepare_b_kernel(place, b_ref, keep_ref, pass_ref):
    c, y, x = place[1], place[2], place[3]
    width = keep_ref.shape[2] // N
    for core, ref in ((c, keep_ref), (1 - c, pass_ref)):
        for g in range(N):
            for i, h in enumerate(ORDER):
                ty = lax.rem(y + g * (1 - core) + h * core, N)
                tx = lax.rem(x + g * core + h * (1 - core), N)
                start = pl.multiple_of(((ty * N + tx) * 2 + core) * width, width)
                ref[g, :, i * width : (i + 1) * width] = b_ref[:, pl.ds(start, width)]


def prepare_b(b, place):
    rows, columns = b.shape
    part = jax.ShapeDtypeStruct((N, rows, columns // (2 * N)), b.dtype)
    return pl.pallas_call(
        prepare_b_kernel,
        out_shape=(part, part),
        in_specs=[SMEM, VMEM],
        out_specs=(VMEM, VMEM),
        compiler_params=PARAMS,
        name="prepare_b",
    )(place, b)


def join_a_kernel(side, got, out_ref):
    rows = side.shape[1]
    out_ref[:, :rows] = side[...]
    out_ref[:, rows:] = got[1]


def join_a(side, got):
    _, rows, half = side.shape
    return pl.pallas_call(
        join_a_kernel,
        out_shape=jax.ShapeDtypeStruct((2, 2 * rows, half), side.dtype),
        in_specs=[VMEM] * 2,
        out_specs=VMEM,
        compiler_params=PARAMS,
        name="join_a",
    )(side, got)


def join_b_kernel(keep, got, *refs):
    rows = keep.shape[1]
    for g, ref in enumerate(refs):
        ref[:rows] = keep[g]
        ref[rows:] = got[g]


def join_b(keep, got):
    _, rows, columns = keep.shape
    return pl.pallas_call(
        join_b_kernel,
        out_shape=(jax.ShapeDtypeStruct((2 * rows, columns), keep.dtype),) * N,
        in_specs=[VMEM] * 2,
        out_specs=(VMEM,) * N,
        compiler_params=PARAMS,
        name="join_b",
    )(keep, got)


def panel_kernel(*refs):
    out_refs = refs[N:]
    width = out_refs[0].shape[2]
    for g in range(N):
        for part, ref in enumerate(out_refs):
            ref[g] = refs[g][:, part * width : (part + 1) * width]


def make_panels(blocks):
    rows, columns = blocks[0].shape
    out = jax.ShapeDtypeStruct((N, rows, columns // STREAMS), blocks[0].dtype)
    return pl.pallas_call(
        panel_kernel,
        out_shape=(out,) * STREAMS,
        in_specs=[VMEM] * N,
        out_specs=(VMEM,) * STREAMS,
        compiler_params=PARAMS,
        name="panel",
    )(*blocks)


def stack_kernel(own, got, side, two, two_got, side_got, *out_refs):
    rows = two.shape[1]
    for part, ref in enumerate(out_refs):
        blocks = [
            own[part],
            got[0, part],
            side[part, :rows],
            side[part, rows:],
            two[part],
            two_got[1 - part],
            side_got[1 - part, rows:],
            side_got[1 - part, :rows],
        ]
        for i, block in enumerate(blocks):
            ref[i * rows : (i + 1) * rows] = block


def stack(own, got, side, two, two_got, side_got):
    _, rows, half = two.shape
    out = jax.ShapeDtypeStruct((2 * N * rows, half), two.dtype)
    return pl.pallas_call(
        stack_kernel,
        out_shape=(out, out),
        in_specs=[VMEM] * 6,
        out_specs=(VMEM, VMEM),
        compiler_params=PARAMS,
        name="stack",
    )(own, got, side, two, two_got, side_got)


NEAR = 3


def split_a_kernel(*refs):
    high_ref, low_ref = refs[2 * NEAR :]
    for i in range(2 * NEAR):
        depth = refs[i].shape[0]
        place = slice(i % NEAR * depth, (i % NEAR + 1) * depth)
        high_ref[i // NEAR, :, place], low_ref[i // NEAR, :, place] = split(refs[i][...].T)


def split_a(tops, bottoms):
    depth, columns = tops[0].shape
    out = jax.ShapeDtypeStruct((2, columns, NEAR * depth), jnp.bfloat16)
    return pl.pallas_call(
        split_a_kernel,
        out_shape=(out, out),
        in_specs=[VMEM] * (2 * NEAR),
        out_specs=(VMEM, VMEM),
        compiler_params=PARAMS,
        name="split_a",
    )(*tops, *bottoms)


def split_b_kernel(*refs):
    high_ref, low_ref = refs[N:]
    slab = refs[0].shape[1]
    for i, g in enumerate((0, 1, 3, 2)):
        for s in range(N):
            place = slice((i * N + s) * slab, (i * N + s + 1) * slab)
            high_ref[place], low_ref[place] = split(refs[s][g])


def split_b(panels):
    _, slab, columns = panels[0].shape
    out = jax.ShapeDtypeStruct((N * N * slab, columns), jnp.bfloat16)
    return pl.pallas_call(
        split_b_kernel,
        out_shape=(out, out),
        in_specs=[VMEM] * N,
        out_specs=(VMEM, VMEM),
        compiler_params=PARAMS,
        name="split_b",
    )(*panels)


TILE = 512
WEIGHT = 2


def three_products(high, low, bh, bl):
    return dot(high, bh) + dot(high, bl) + dot(low, bh)


def near_kernel(high, low, bh, bl, *out_refs):
    depth = high.shape[2]
    for half, ref in enumerate(out_refs):
        rows, width = ref.shape
        for start in range(0, rows, TILE):
            tile = slice(start, start + TILE)
            ref[tile] = three_products(
                high[half, tile], low[half, tile], bh[:depth, :width], bl[:depth, :width]
            )


def first_kernel(top, bottom, near_top, near_bottom, bh, bl, far_high, far_low, *out_refs):
    depth = far_high.shape[2]
    rest = slice(bh.shape[0] - depth, bh.shape[0])
    for half, (far, near, ref) in enumerate(zip((top, bottom), (near_top, near_bottom), out_refs)):
        rows, width = ref.shape
        far_high[half], far_low[half] = split(far[...].T)
        for start in range(0, rows, TILE):
            tile = slice(start, start + TILE)
            ref[tile] = near[tile] + three_products(
                far_high[half, tile], far_low[half, tile], bh[rest, :width], bl[rest, :width]
            )


def product_kernel(tasks, high, low, far_high, far_low, *refs):
    near = high.shape[2]
    b_refs, out_refs = refs[: 2 * STREAMS], refs[2 * STREAMS :]
    for (half, place), ref in zip(tasks, out_refs):
        rows, width = ref.shape
        which, place = divmod(place, N // STREAMS)
        h, l = b_refs[2 * which : 2 * which + 2]
        columns = slice(place * width, (place + 1) * width)
        for start in range(0, rows, TILE):
            tile = slice(start, start + TILE)
            ref[tile] = three_products(
                high[half, tile], low[half, tile], h[:near, columns], l[:near, columns]
            ) + three_products(
                far_high[half, tile], far_low[half, tile], h[near:, columns], l[near:, columns]
            )


def cost(rows, depth, width):
    return pl.CostEstimate(
        flops=12 * rows * depth * width, bytes_accessed=8 * rows * width, transcendentals=0
    )


def near_product(high, low, bh, bl):
    _, rows, depth = high.shape
    width = bh.shape[1] * STREAMS // N
    out = jax.ShapeDtypeStruct((rows, width), jnp.float32)
    return pl.pallas_call(
        near_kernel,
        out_shape=(out, out),
        in_specs=[VMEM] * 4,
        out_specs=(VMEM,) * 2,
        compiler_params=PARAMS,
        cost_estimate=cost(rows, WEIGHT * depth, width),
        name="near_product",
    )(high, low, bh, bl)


def first_product(top, bottom, near_top, near_bottom, bh, bl):
    depth, rows = top.shape
    width = bh.shape[1] * STREAMS // N
    far = jax.ShapeDtypeStruct((2, rows, depth), jnp.bfloat16)
    out = jax.ShapeDtypeStruct((rows, width), jnp.float32)
    return pl.pallas_call(
        first_kernel,
        out_shape=(far, far, out, out),
        in_specs=[VMEM] * 6,
        out_specs=(VMEM,) * 4,
        compiler_params=PARAMS,
        cost_estimate=cost(rows, depth, width),
        name="first_product",
    )(top, bottom, near_top, near_bottom, bh, bl)


def product(tasks, high, low, far_high, far_low, *b):
    _, rows, depth = far_high.shape
    width = b[0].shape[1] * STREAMS // N
    out = jax.ShapeDtypeStruct((rows, width), jnp.float32)
    tasks = tuple((half, ORDER.index(r)) for half, r in tasks)
    return pl.pallas_call(
        functools.partial(product_kernel, tasks),
        out_shape=(out, out),
        in_specs=[VMEM] * (4 + 2 * STREAMS),
        out_specs=(VMEM,) * 2,
        compiler_params=PARAMS,
        cost_estimate=cost(rows, N * depth, width),
        name="product",
    )(high, low, far_high, far_low, *b)


def finish_kernel(place, top0, top3, top1, got, out_ref, mine, sems):
    rows, width = top0.shape
    tile = rows // 4
    copies = []
    for i in range(4):
        tile_rows = slice(i * tile, (i + 1) * tile)
        mine[tile_rows] = top0[tile_rows] + top3[tile_rows] + top1[tile_rows]
        for k, ref, core in ((0, mine, place[1]), (1, got, 1 - place[1])):
            start = pl.multiple_of(core * width, width)
            copy = pltpu.make_async_copy(
                ref.at[tile_rows], out_ref.at[tile_rows, pl.ds(start, width)], sems.at[k, i]
            )
            copy.start()
            copies.append(copy)
    for copy in copies:
        copy.wait()


def finish(place, top0, top3, top1, got):
    rows, width = top0.shape
    return pl.pallas_call(
        finish_kernel,
        out_shape=jax.ShapeDtypeStruct((rows, 2 * width), jnp.float32),
        in_specs=[SMEM] + [VMEM] * 4,
        out_specs=HBM,
        scratch_shapes=[pltpu.VMEM((rows, width), jnp.float32), pltpu.SemaphoreType.DMA((2, 4))],
        compiler_params=PARAMS,
        name="finish",
    )(place, top0, top3, top1, got)


TOP, BOTTOM = 0, 1


def shards(a, b):
    place = jnp.stack([lax.axis_index(name) for name in ALL]).astype(jnp.int32)

    own, two, side, handed = prepare_a(a, place)
    two = along_z(two, 2)
    got = swap(handed)
    side = along_z(join_a(side, got), 1)

    keep, give = prepare_b(b, place)
    blocks = join_b(keep, swap(give))
    blocks = [blocks[0]] + [along_gather(blocks[g], g) for g in range(1, N)]
    two, side, blocks = lax.optimization_barrier((two, side, blocks))

    two_got, side_got = swap(two), swap(side)
    panels = make_panels(blocks)
    two_got, side_got, panels = lax.optimization_barrier((two_got, side_got, panels))
    streams = [[panel] for panel in panels]
    for _ in range(N - 1):
        for stream in streams:
            stream.append(along_z(stream[-1], 1))

    top, bottom = stack(own, got, side, two, two_got, side_got)
    top_behind = along_gather(top, 1)
    bottom_ahead = along_gather(bottom, -1)
    bottom_behind = along_gather(bottom, 1)
    top_ahead = along_gather(top, -1)
    top_far = along_gather(top_behind, 1)
    bottom_far = along_gather(bottom_ahead, -1)

    high, low = split_a((top, top_behind, top_ahead), (bottom, bottom_behind, bottom_ahead))
    splits = [half for stream in streams for half in split_b(stream)]
    near = near_product(high, low, *splits[:2])
    far_high, far_low, top2, bottom2 = first_product(top_far, bottom_far, *near, *splits[:2])
    operands = (high, low, far_high, far_low, *splits)
    bottom1, top3 = product(((BOTTOM, 1), (TOP, 3)), *operands)
    top1, bottom3 = product(((TOP, 1), (BOTTOM, 3)), *operands)

    top2 = along_reduce(top2, 1)
    bottom2 = along_reduce(bottom2, -1)
    top2, bottom2, operands = lax.optimization_barrier((top2, bottom2, operands))
    bottom1 = along_reduce(bottom1, 1)
    top3 = along_reduce(top3, -1)
    top1 = along_reduce(top1 + top2, 1)
    bottom3 = along_reduce(bottom3 + bottom2, -1)
    top0, bottom0 = product(((TOP, 0), (BOTTOM, 0)), *operands)
    got = swap(bottom0 + bottom1 + bottom3)
    return finish(place, top0, top3, top1, got)


def solution(mesh):
    fine = Mesh(mesh.devices.reshape(N, 2, N, N), ALL)
    return jax.shard_map(
        shards,
        mesh=fine,
        in_specs=(P(ALL, None), P(ALL, None)),
        out_specs=P(("z", "c"), ("y", "x")),
        check_vma=False,
    )
```

```python
import functools
import itertools

import jax
import jax.numpy as jnp
from jax import lax
from jax.experimental import pallas as pl
from jax.experimental.pallas import tpu as pltpu
from jax.sharding import Mesh, PartitionSpec as P

N = 4
ALL = ("z", "c", "y", "x")
VMEM_LIMIT = 16 * 1024 * 1024


def permute(value, target):
    pairs = []
    for z, c, y, x in itertools.product(range(N), range(2), range(N), range(N)):
        tz, tc, ty, tx = target(z, c, y, x)
        place = ((tz % N * 2 + tc % 2) * N + ty % N) * N + tx % N
        pairs.append((((z * 2 + c) * N + y) * N + x, place))
    return lax.ppermute(value, ALL, pairs)


def swap(value):
    return permute(value, lambda z, c, y, x: (z, 1 - c, y, x))


def along_z(value, step):
    return permute(value, lambda z, c, y, x: (z + step * (1 - 2 * c), c, y, x))


def along_gather(value, step):
    return permute(value, lambda z, c, y, x: (z, c, y + step * (1 - c), x + step * c))


def along_reduce(value, step):
    return permute(value, lambda z, c, y, x: (z, c, y + step * c, x + step * (1 - c)))


def split(value):
    high = value.astype(jnp.bfloat16)
    low = (value - high.astype(jnp.float32)).astype(jnp.bfloat16)
    return high, low


def dot(first, second):
    return lax.dot_general(
        first, second, (((1,), (0,)), ((), ())), preferred_element_type=jnp.float32
    )


SMEM = pl.BlockSpec(memory_space=pltpu.SMEM)
VMEM = pl.BlockSpec(memory_space=pltpu.VMEM)
ANY = pl.BlockSpec(memory_space=pl.ANY)
HBM = pl.BlockSpec(memory_space=pltpu.HBM)
PARAMS = pltpu.CompilerParams(vmem_limit_bytes=VMEM_LIMIT)


def prepare_a_kernel(place, a_ref, own_ref, two_ref, side_ref, pass_ref):
    z, c = place[0], place[1]
    half = own_ref.shape[2]

    def piece(step, part):
        start = (lax.rem(z + step, N) * 2 + part) * half
        return a_ref[:, pl.ds(pl.multiple_of(start, half), half)]

    for part in range(2):
        mine = lax.rem(c + part, 2)
        own_ref[part] = piece(0, mine)
        two_ref[part] = piece(2, mine)
        side_ref[part] = piece(1 + 2 * c, mine)
        pass_ref[0, part] = piece(0, 1 - mine)
        pass_ref[1, part] = piece(3 - 2 * c, 1 - mine)


def prepare_a(a, place):
    rows, columns = a.shape
    piece = jax.ShapeDtypeStruct((2, rows, columns // (2 * N)), a.dtype)
    passed = jax.ShapeDtypeStruct((2, 2, rows, columns // (2 * N)), a.dtype)
    return pl.pallas_call(
        prepare_a_kernel,
        out_shape=(piece, piece, piece, passed),
        in_specs=[SMEM, VMEM],
        out_specs=(VMEM,) * 4,
        compiler_params=PARAMS,
        name="prepare_a",
    )(place, a)


AHEAD = 3
ORDER = (2, 1, 3, 0)


def prepare_b_kernel(place, b_ref, keep_ref, pass_ref):
    c, y, x = place[1], place[2], place[3]
    width = keep_ref.shape[2] // N
    for core, ref in ((c, keep_ref), (1 - c, pass_ref)):
        for g in range(N):
            for i, h in enumerate(ORDER):
                ty = lax.rem(y + g * (1 - core) + h * core, N)
                tx = lax.rem(x + g * core + h * (1 - core), N)
                start = pl.multiple_of(((ty * N + tx) * 2 + core) * width, width)
                ref[g, :, i * width : (i + 1) * width] = b_ref[:, pl.ds(start, width)]


def prepare_b(b, place):
    rows, columns = b.shape
    part = jax.ShapeDtypeStruct((N, rows, columns // (2 * N)), b.dtype)
    return pl.pallas_call(
        prepare_b_kernel,
        out_shape=(part, part),
        in_specs=[SMEM, VMEM],
        out_specs=(VMEM, VMEM),
        compiler_params=PARAMS,
        name="prepare_b",
    )(place, b)


def join_a_kernel(side, got, out_ref):
    rows = side.shape[1]
    out_ref[:, :rows] = side[...]
    out_ref[:, rows:] = got[1]


def join_a(side, got):
    _, rows, half = side.shape
    return pl.pallas_call(
        join_a_kernel,
        out_shape=jax.ShapeDtypeStruct((2, 2 * rows, half), side.dtype),
        in_specs=[VMEM] * 2,
        out_specs=VMEM,
        compiler_params=PARAMS,
        name="join_a",
    )(side, got)


def join_b_kernel(keep, got, *refs):
    rows = keep.shape[1]
    for g, ref in enumerate(refs):
        ref[:rows] = keep[g]
        ref[rows:] = got[g]


def join_b(keep, got):
    _, rows, columns = keep.shape
    return pl.pallas_call(
        join_b_kernel,
        out_shape=(jax.ShapeDtypeStruct((2 * rows, columns), keep.dtype),) * N,
        in_specs=[VMEM] * 2,
        out_specs=(VMEM,) * N,
        compiler_params=PARAMS,
        name="join_b",
    )(keep, got)


def panel_kernel(*refs):
    out_refs = refs[N:]
    width = out_refs[0].shape[2]
    for g in range(N):
        out_refs[0][g] = refs[g][:, :width]
        out_refs[1][g] = refs[g][:, width:]


def make_panels(blocks):
    rows, columns = blocks[0].shape
    width = columns * AHEAD // N
    return pl.pallas_call(
        panel_kernel,
        out_shape=(
            jax.ShapeDtypeStruct((N, rows, width), blocks[0].dtype),
            jax.ShapeDtypeStruct((N, rows, columns - width), blocks[0].dtype),
        ),
        in_specs=[VMEM] * N,
        out_specs=(VMEM, VMEM),
        compiler_params=PARAMS,
        name="panel",
    )(*blocks)


def stack_kernel(own, got, side, two, two_got, side_got, *out_refs):
    rows = two.shape[1]
    for part, ref in enumerate(out_refs):
        blocks = [
            own[part],
            got[0, part],
            side[part, :rows],
            side[part, rows:],
            two[part],
            two_got[1 - part],
            side_got[1 - part, rows:],
            side_got[1 - part, :rows],
        ]
        for i, block in enumerate(blocks):
            ref[i * rows : (i + 1) * rows] = block


def stack(own, got, side, two, two_got, side_got):
    _, rows, half = two.shape
    out = jax.ShapeDtypeStruct((2 * N * rows, half), two.dtype)
    return pl.pallas_call(
        stack_kernel,
        out_shape=(out, out),
        in_specs=[VMEM] * 6,
        out_specs=(VMEM, VMEM),
        compiler_params=PARAMS,
        name="stack",
    )(own, got, side, two, two_got, side_got)


NEAR = 3


def split_a_kernel(*refs):
    high_ref, low_ref = refs[2 * NEAR :]
    for i in range(2 * NEAR):
        depth = refs[i].shape[0]
        place = slice(i % NEAR * depth, (i % NEAR + 1) * depth)
        high_ref[i // NEAR, :, place], low_ref[i // NEAR, :, place] = split(refs[i][...].T)


def split_a(tops, bottoms):
    depth, columns = tops[0].shape
    out = jax.ShapeDtypeStruct((2, columns, NEAR * depth), jnp.bfloat16)
    return pl.pallas_call(
        split_a_kernel,
        out_shape=(out, out),
        in_specs=[VMEM] * (2 * NEAR),
        out_specs=(VMEM, VMEM),
        compiler_params=PARAMS,
        name="split_a",
    )(*tops, *bottoms)


def split_b_kernel(*refs):
    high_ref, low_ref = refs[N:]
    slab = refs[0].shape[1]
    for i, g in enumerate((0, 1, 3, 2)):
        for s in range(N):
            place = slice((i * N + s) * slab, (i * N + s + 1) * slab)
            high_ref[place], low_ref[place] = split(refs[s][g])


def split_b(panels):
    _, slab, columns = panels[0].shape
    out = jax.ShapeDtypeStruct((N * N * slab, columns), jnp.bfloat16)
    return pl.pallas_call(
        split_b_kernel,
        out_shape=(out, out),
        in_specs=[VMEM] * N,
        out_specs=(VMEM, VMEM),
        compiler_params=PARAMS,
        name="split_b",
    )(*panels)


TILE = 512


def three_products(high, low, bh, bl):
    return dot(high, bh) + dot(high, bl) + dot(low, bh)


def near_kernel(high, low, bh, bl, *out_refs):
    depth = high.shape[2]
    for half, ref in enumerate(out_refs):
        rows, width = ref.shape
        for start in range(0, rows, TILE):
            tile = slice(start, start + TILE)
            ref[tile] = three_products(
                high[half, tile], low[half, tile], bh[:depth, :width], bl[:depth, :width]
            )


def first_kernel(top, bottom, near_top, near_bottom, bh, bl, far_high, far_low, *out_refs):
    depth = far_high.shape[2]
    rest = slice(bh.shape[0] - depth, bh.shape[0])
    for half, (far, near, ref) in enumerate(zip((top, bottom), (near_top, near_bottom), out_refs)):
        rows, width = ref.shape
        far_high[half], far_low[half] = split(far[...].T)
        for start in range(0, rows, TILE):
            tile = slice(start, start + TILE)
            ref[tile] = near[tile] + three_products(
                far_high[half, tile], far_low[half, tile], bh[rest, :width], bl[rest, :width]
            )


def product_kernel(tasks, high, low, far_high, far_low, bh, bl, *out_refs):
    near = high.shape[2]
    for (half, place), ref in zip(tasks, out_refs):
        rows, width = ref.shape
        columns = slice(place * width, (place + 1) * width)
        for start in range(0, rows, TILE):
            tile = slice(start, start + TILE)
            ref[tile] = three_products(
                high[half, tile], low[half, tile], bh[:near, columns], bl[:near, columns]
            ) + three_products(
                far_high[half, tile], far_low[half, tile], bh[near:, columns], bl[near:, columns]
            )


def cost(rows, depth, width):
    return pl.CostEstimate(
        flops=12 * rows * depth * width, bytes_accessed=8 * rows * width, transcendentals=0
    )


def near_product(high, low, bh, bl):
    _, rows, depth = high.shape
    width = bh.shape[1] // AHEAD
    out = jax.ShapeDtypeStruct((rows, width), jnp.float32)
    return pl.pallas_call(
        near_kernel,
        out_shape=(out, out),
        in_specs=[VMEM] * 4,
        out_specs=(VMEM,) * 2,
        compiler_params=PARAMS,
        cost_estimate=cost(rows, depth, width),
        name="near_product",
    )(high, low, bh, bl)


def first_product(top, bottom, near_top, near_bottom, bh, bl):
    depth, rows = top.shape
    width = bh.shape[1] // AHEAD
    far = jax.ShapeDtypeStruct((2, rows, depth), jnp.bfloat16)
    out = jax.ShapeDtypeStruct((rows, width), jnp.float32)
    return pl.pallas_call(
        first_kernel,
        out_shape=(far, far, out, out),
        in_specs=[VMEM] * 6,
        out_specs=(VMEM,) * 4,
        compiler_params=PARAMS,
        cost_estimate=cost(rows, depth, width),
        name="first_product",
    )(top, bottom, near_top, near_bottom, bh, bl)


def product(r, high, low, far_high, far_low, bh, bl):
    _, rows, depth = far_high.shape
    place = ORDER.index(r)
    width = bh.shape[1] // (AHEAD if place < AHEAD else N - AHEAD)
    out = jax.ShapeDtypeStruct((rows, width), jnp.float32)
    tasks = ((TOP, place % AHEAD), (BOTTOM, place % AHEAD))
    return pl.pallas_call(
        functools.partial(product_kernel, tasks),
        out_shape=(out, out),
        in_specs=[VMEM] * 6,
        out_specs=(VMEM,) * 2,
        compiler_params=PARAMS,
        cost_estimate=cost(rows, N * depth, width),
        name="product",
    )(high, low, far_high, far_low, bh, bl)


def finish_kernel(place, top0, top3, top1, got, out_ref, mine, sems):
    rows, width = top0.shape
    tile = rows // 4
    copies = []
    for i in range(4):
        tile_rows = slice(i * tile, (i + 1) * tile)
        mine[tile_rows] = top0[tile_rows] + top3[tile_rows] + top1[tile_rows]
        for k, ref, core in ((0, mine, place[1]), (1, got, 1 - place[1])):
            start = pl.multiple_of(core * width, width)
            copy = pltpu.make_async_copy(
                ref.at[tile_rows], out_ref.at[tile_rows, pl.ds(start, width)], sems.at[k, i]
            )
            copy.start()
            copies.append(copy)
    for copy in copies:
        copy.wait()


def finish(place, top0, top3, top1, got):
    rows, width = top0.shape
    return pl.pallas_call(
        finish_kernel,
        out_shape=jax.ShapeDtypeStruct((rows, 2 * width), jnp.float32),
        in_specs=[SMEM] + [VMEM] * 4,
        out_specs=HBM,
        scratch_shapes=[pltpu.VMEM((rows, width), jnp.float32), pltpu.SemaphoreType.DMA((2, 4))],
        compiler_params=PARAMS,
        name="finish",
    )(place, top0, top3, top1, got)


TOP, BOTTOM = 0, 1


def shards(a, b):
    place = jnp.stack([lax.axis_index(name) for name in ALL]).astype(jnp.int32)

    own, two, side, handed = prepare_a(a, place)
    two = along_z(two, 2)
    got = swap(handed)
    side = along_z(join_a(side, got), 1)

    keep, give = prepare_b(b, place)
    blocks = join_b(keep, swap(give))
    blocks = [blocks[0]] + [along_gather(blocks[g], g) for g in range(1, N)]
    two, side, blocks = lax.optimization_barrier((two, side, blocks))

    two_got, side_got = swap(two), swap(side)
    panels = make_panels(blocks)
    two_got, side_got, panels = lax.optimization_barrier((two_got, side_got, panels))
    panels, later = [panels[0]], [panels[1]]
    for _ in range(N - 1):
        panels.append(along_z(panels[-1], 1))
    panels[-1], later[0] = lax.optimization_barrier((panels[-1], later[0]))
    later.append(along_z(later[-1], 1))

    top, bottom = stack(own, got, side, two, two_got, side_got)
    top_behind = along_gather(top, 1)
    bottom_ahead = along_gather(bottom, -1)
    bottom_behind = along_gather(bottom, 1)
    top_ahead = along_gather(top, -1)
    top_far = along_gather(top_behind, 1)
    bottom_far = along_gather(bottom_ahead, -1)

    high, low = split_a((top, top_behind, top_ahead), (bottom, bottom_behind, bottom_ahead))
    bh, bl = split_b(panels)
    near = near_product(high, low, bh, bl)
    far_high, far_low, top2, bottom2 = first_product(top_far, bottom_far, *near, bh, bl)
    _, later[1] = lax.optimization_barrier((top2, later[1]))
    later.append(along_z(later[-1], 1))
    halves = (high, low, far_high, far_low)
    top1, bottom1 = product(1, *halves, bh, bl)
    top3, bottom3 = product(3, *halves, bh, bl)

    top2 = along_reduce(top2, 1)
    bottom2 = along_reduce(bottom2, -1)
    _, later[2] = lax.optimization_barrier((top2, later[2]))
    bottom1 = along_reduce(bottom1, 1)
    top3 = along_reduce(top3, -1)
    top1 = along_reduce(top1 + top2, 1)
    bottom3 = along_reduce(bottom3 + bottom2, -1)
    later.append(along_z(later[-1], 1))
    top0, bottom0 = product(0, *halves, *split_b(later))
    got = swap(bottom0 + bottom1 + bottom3)
    return finish(place, top0, top3, top1, got)


def solution(mesh):
    fine = Mesh(mesh.devices.reshape(N, 2, N, N), ALL)
    return jax.shard_map(
        shards,
        mesh=fine,
        in_specs=(P(ALL, None), P(ALL, None)),
        out_specs=P(("z", "c"), ("y", "x")),
        check_vma=False,
    )
```

```python
import functools
import itertools

import jax
import jax.numpy as jnp
from jax import lax
from jax.experimental import pallas as pl
from jax.experimental.pallas import tpu as pltpu
from jax.sharding import Mesh, PartitionSpec as P

N = 4
ALL = ("z", "c", "y", "x")
VMEM_LIMIT = 16 * 1024 * 1024


def permute(value, target):
    pairs = []
    for z, c, y, x in itertools.product(range(N), range(2), range(N), range(N)):
        tz, tc, ty, tx = target(z, c, y, x)
        place = ((tz % N * 2 + tc % 2) * N + ty % N) * N + tx % N
        pairs.append((((z * 2 + c) * N + y) * N + x, place))
    return lax.ppermute(value, ALL, pairs)


def swap(value):
    return permute(value, lambda z, c, y, x: (z, 1 - c, y, x))


def along_z(value, step):
    return permute(value, lambda z, c, y, x: (z + step * (1 - 2 * c), c, y, x))


def along_gather(value, step):
    return permute(value, lambda z, c, y, x: (z, c, y + step * (1 - c), x + step * c))


def along_reduce(value, step):
    return permute(value, lambda z, c, y, x: (z, c, y + step * c, x + step * (1 - c)))


def split(value):
    high = value.astype(jnp.bfloat16)
    low = (value - high.astype(jnp.float32)).astype(jnp.bfloat16)
    return high, low


def dot(first, second):
    return lax.dot_general(
        first, second, (((1,), (0,)), ((), ())), preferred_element_type=jnp.float32
    )


SMEM = pl.BlockSpec(memory_space=pltpu.SMEM)
VMEM = pl.BlockSpec(memory_space=pltpu.VMEM)
ANY = pl.BlockSpec(memory_space=pl.ANY)
HBM = pl.BlockSpec(memory_space=pltpu.HBM)
PARAMS = pltpu.CompilerParams(vmem_limit_bytes=VMEM_LIMIT)


def prepare_a_kernel(place, a_ref, own_ref, two_ref, side_ref, pass_ref):
    z, c = place[0], place[1]
    half = own_ref.shape[2]

    def piece(step, part):
        start = (lax.rem(z + step, N) * 2 + part) * half
        return a_ref[:, pl.ds(pl.multiple_of(start, half), half)]

    for part in range(2):
        mine = lax.rem(c + part, 2)
        own_ref[part] = piece(0, mine)
        two_ref[part] = piece(2, mine)
        side_ref[part] = piece(1 + 2 * c, mine)
        pass_ref[0, part] = piece(0, 1 - mine)
        pass_ref[1, part] = piece(3 - 2 * c, 1 - mine)


def prepare_a(a, place):
    rows, columns = a.shape
    piece = jax.ShapeDtypeStruct((2, rows, columns // (2 * N)), a.dtype)
    passed = jax.ShapeDtypeStruct((2, 2, rows, columns // (2 * N)), a.dtype)
    return pl.pallas_call(
        prepare_a_kernel,
        out_shape=(piece, piece, piece, passed),
        in_specs=[SMEM, VMEM],
        out_specs=(VMEM,) * 4,
        compiler_params=PARAMS,
        name="prepare_a",
    )(place, a)


AHEAD = 3
ORDER = (2, 3, 1, 0)


def prepare_b_kernel(place, b_ref, keep_ref, pass_ref):
    c, y, x = place[1], place[2], place[3]
    width = keep_ref.shape[2] // N
    for core, ref in ((c, keep_ref), (1 - c, pass_ref)):
        for g in range(N):
            for i, h in enumerate(ORDER):
                ty = lax.rem(y + g * (1 - core) + h * core, N)
                tx = lax.rem(x + g * core + h * (1 - core), N)
                start = pl.multiple_of(((ty * N + tx) * 2 + core) * width, width)
                ref[g, :, i * width : (i + 1) * width] = b_ref[:, pl.ds(start, width)]


def prepare_b(b, place):
    rows, columns = b.shape
    part = jax.ShapeDtypeStruct((N, rows, columns // (2 * N)), b.dtype)
    return pl.pallas_call(
        prepare_b_kernel,
        out_shape=(part, part),
        in_specs=[SMEM, VMEM],
        out_specs=(VMEM, VMEM),
        compiler_params=PARAMS,
        name="prepare_b",
    )(place, b)


def join_a_kernel(side, got, out_ref):
    rows = side.shape[1]
    out_ref[:, :rows] = side[...]
    out_ref[:, rows:] = got[1]


def join_a(side, got):
    _, rows, half = side.shape
    return pl.pallas_call(
        join_a_kernel,
        out_shape=jax.ShapeDtypeStruct((2, 2 * rows, half), side.dtype),
        in_specs=[VMEM] * 2,
        out_specs=VMEM,
        compiler_params=PARAMS,
        name="join_a",
    )(side, got)


def join_b_kernel(keep, got, *refs):
    rows = keep.shape[1]
    for g, ref in enumerate(refs):
        ref[:rows] = keep[g]
        ref[rows:] = got[g]


def join_b(keep, got):
    _, rows, columns = keep.shape
    return pl.pallas_call(
        join_b_kernel,
        out_shape=(jax.ShapeDtypeStruct((2 * rows, columns), keep.dtype),) * N,
        in_specs=[VMEM] * 2,
        out_specs=(VMEM,) * N,
        compiler_params=PARAMS,
        name="join_b",
    )(keep, got)


def panel_kernel(*refs):
    out_refs = refs[N:]
    width = out_refs[0].shape[2]
    for g in range(N):
        out_refs[0][g] = refs[g][:, :width]
        out_refs[1][g] = refs[g][:, width:]


def make_panels(blocks):
    rows, columns = blocks[0].shape
    width = columns * AHEAD // N
    return pl.pallas_call(
        panel_kernel,
        out_shape=(
            jax.ShapeDtypeStruct((N, rows, width), blocks[0].dtype),
            jax.ShapeDtypeStruct((N, rows, columns - width), blocks[0].dtype),
        ),
        in_specs=[VMEM] * N,
        out_specs=(VMEM, VMEM),
        compiler_params=PARAMS,
        name="panel",
    )(*blocks)


def stack_kernel(own, got, side, two, two_got, side_got, *out_refs):
    rows = two.shape[1]
    for part, ref in enumerate(out_refs):
        blocks = [
            own[part],
            got[0, part],
            side[part, :rows],
            side[part, rows:],
            two[part],
            two_got[1 - part],
            side_got[1 - part, rows:],
            side_got[1 - part, :rows],
        ]
        for i, block in enumerate(blocks):
            ref[i * rows : (i + 1) * rows] = block


def stack(own, got, side, two, two_got, side_got):
    _, rows, half = two.shape
    out = jax.ShapeDtypeStruct((2 * N * rows, half), two.dtype)
    return pl.pallas_call(
        stack_kernel,
        out_shape=(out, out),
        in_specs=[VMEM] * 6,
        out_specs=(VMEM, VMEM),
        compiler_params=PARAMS,
        name="stack",
    )(own, got, side, two, two_got, side_got)


NEAR = 3


def split_a_kernel(*refs):
    high_ref, low_ref = refs[2 * NEAR :]
    for i in range(2 * NEAR):
        depth = refs[i].shape[0]
        place = slice(i % NEAR * depth, (i % NEAR + 1) * depth)
        high_ref[i // NEAR, :, place], low_ref[i // NEAR, :, place] = split(refs[i][...].T)


def split_a(tops, bottoms):
    depth, columns = tops[0].shape
    out = jax.ShapeDtypeStruct((2, columns, NEAR * depth), jnp.bfloat16)
    return pl.pallas_call(
        split_a_kernel,
        out_shape=(out, out),
        in_specs=[VMEM] * (2 * NEAR),
        out_specs=(VMEM, VMEM),
        compiler_params=PARAMS,
        name="split_a",
    )(*tops, *bottoms)


def split_b_kernel(*refs):
    high_ref, low_ref = refs[N:]
    slab = refs[0].shape[1]
    for i, g in enumerate((0, 1, 3, 2)):
        for s in range(N):
            place = slice((i * N + s) * slab, (i * N + s + 1) * slab)
            high_ref[place], low_ref[place] = split(refs[s][g])


def split_b(panels):
    _, slab, columns = panels[0].shape
    out = jax.ShapeDtypeStruct((N * N * slab, columns), jnp.bfloat16)
    return pl.pallas_call(
        split_b_kernel,
        out_shape=(out, out),
        in_specs=[VMEM] * N,
        out_specs=(VMEM, VMEM),
        compiler_params=PARAMS,
        name="split_b",
    )(*panels)


TILE = 512


def three_products(high, low, bh, bl):
    return dot(high, bh) + dot(high, bl) + dot(low, bh)


def near_kernel(high, low, bh, bl, *out_refs):
    depth = high.shape[2]
    for half, ref in enumerate(out_refs):
        rows, width = ref.shape
        for start in range(0, rows, TILE):
            tile = slice(start, start + TILE)
            ref[tile] = three_products(
                high[half, tile], low[half, tile], bh[:depth, :width], bl[:depth, :width]
            )


def first_kernel(top, bottom, near_top, near_bottom, bh, bl, far_high, far_low, *out_refs):
    depth = far_high.shape[2]
    rest = slice(bh.shape[0] - depth, bh.shape[0])
    for half, (far, near, ref) in enumerate(zip((top, bottom), (near_top, near_bottom), out_refs)):
        rows, width = ref.shape
        far_high[half], far_low[half] = split(far[...].T)
        for start in range(0, rows, TILE):
            tile = slice(start, start + TILE)
            ref[tile] = near[tile] + three_products(
                far_high[half, tile], far_low[half, tile], bh[rest, :width], bl[rest, :width]
            )


def product_kernel(tasks, high, low, far_high, far_low, bh, bl, *out_refs):
    near = high.shape[2]
    for (half, place), ref in zip(tasks, out_refs):
        rows, width = ref.shape
        columns = slice(place * width, (place + 1) * width)
        for start in range(0, rows, TILE):
            tile = slice(start, start + TILE)
            ref[tile] = three_products(
                high[half, tile], low[half, tile], bh[:near, columns], bl[:near, columns]
            ) + three_products(
                far_high[half, tile], far_low[half, tile], bh[near:, columns], bl[near:, columns]
            )


def cost(rows, depth, width):
    return pl.CostEstimate(
        flops=12 * rows * depth * width, bytes_accessed=8 * rows * width, transcendentals=0
    )


def near_product(high, low, bh, bl):
    _, rows, depth = high.shape
    width = bh.shape[1] // AHEAD
    out = jax.ShapeDtypeStruct((rows, width), jnp.float32)
    return pl.pallas_call(
        near_kernel,
        out_shape=(out, out),
        in_specs=[VMEM] * 4,
        out_specs=(VMEM,) * 2,
        compiler_params=PARAMS,
        cost_estimate=cost(rows, depth, width),
        name="near_product",
    )(high, low, bh, bl)


def first_product(top, bottom, near_top, near_bottom, bh, bl):
    depth, rows = top.shape
    width = bh.shape[1] // AHEAD
    far = jax.ShapeDtypeStruct((2, rows, depth), jnp.bfloat16)
    out = jax.ShapeDtypeStruct((rows, width), jnp.float32)
    return pl.pallas_call(
        first_kernel,
        out_shape=(far, far, out, out),
        in_specs=[VMEM] * 6,
        out_specs=(VMEM,) * 4,
        compiler_params=PARAMS,
        cost_estimate=cost(rows, depth, width),
        name="first_product",
    )(top, bottom, near_top, near_bottom, bh, bl)


def product(r, high, low, far_high, far_low, bh, bl):
    _, rows, depth = far_high.shape
    place = ORDER.index(r)
    width = bh.shape[1] // (AHEAD if place < AHEAD else N - AHEAD)
    out = jax.ShapeDtypeStruct((rows, width), jnp.float32)
    tasks = ((TOP, place % AHEAD), (BOTTOM, place % AHEAD))
    return pl.pallas_call(
        functools.partial(product_kernel, tasks),
        out_shape=(out, out),
        in_specs=[VMEM] * 6,
        out_specs=(VMEM,) * 2,
        compiler_params=PARAMS,
        cost_estimate=cost(rows, N * depth, width),
        name="product",
    )(high, low, far_high, far_low, bh, bl)


def finish_kernel(place, top0, top3, top1, got, out_ref, mine, sems):
    rows, width = top0.shape
    tile = rows // 4
    copies = []
    for k, ref, core in ((1, got, 1 - place[1]), (0, mine, place[1])):
        columns = pl.ds(pl.multiple_of(core * width, width), width)
        for i in range(4):
            tile_rows = slice(i * tile, (i + 1) * tile)
            if k == 0:
                mine[tile_rows] = top0[tile_rows] + top3[tile_rows] + top1[tile_rows]
            copy = pltpu.make_async_copy(
                ref.at[tile_rows], out_ref.at[tile_rows, columns], sems.at[k, i]
            )
            copy.start()
            copies.append(copy)
    for copy in copies:
        copy.wait()


def finish(place, top0, top3, top1, got):
    rows, width = top0.shape
    return pl.pallas_call(
        finish_kernel,
        out_shape=jax.ShapeDtypeStruct((rows, 2 * width), jnp.float32),
        in_specs=[SMEM] + [VMEM] * 4,
        out_specs=HBM,
        scratch_shapes=[pltpu.VMEM((rows, width), jnp.float32), pltpu.SemaphoreType.DMA((2, 4))],
        compiler_params=PARAMS,
        name="finish",
    )(place, top0, top3, top1, got)


TOP, BOTTOM = 0, 1


def shards(a, b):
    place = jnp.stack([lax.axis_index(name) for name in ALL]).astype(jnp.int32)

    own, two, side, handed = prepare_a(a, place)
    two = along_z(two, 2)
    got = swap(handed)
    side = along_z(join_a(side, got), 1)

    keep, give = prepare_b(b, place)
    blocks = join_b(keep, swap(give))
    blocks = [blocks[0]] + [along_gather(blocks[g], g) for g in range(1, N)]
    two, side, blocks = lax.optimization_barrier((two, side, blocks))

    two_got, side_got = swap(two), swap(side)
    panels = make_panels(blocks)
    two_got, side_got, panels = lax.optimization_barrier((two_got, side_got, panels))
    panels, later = [panels[0]], [panels[1]]
    for _ in range(N - 1):
        panels.append(along_z(panels[-1], 1))
    panels[-1], later[0] = lax.optimization_barrier((panels[-1], later[0]))
    later.append(along_z(later[-1], 1))

    top, bottom = stack(own, got, side, two, two_got, side_got)
    top_behind = along_gather(top, 1)
    bottom_ahead = along_gather(bottom, -1)
    bottom_behind = along_gather(bottom, 1)
    top_ahead = along_gather(top, -1)
    top_far = along_gather(top_behind, 1)
    bottom_far = along_gather(bottom_ahead, -1)

    high, low = split_a((top, top_behind, top_ahead), (bottom, bottom_behind, bottom_ahead))
    bh, bl = split_b(panels)
    near = near_product(high, low, bh, bl)
    far_high, far_low, top2, bottom2 = first_product(top_far, bottom_far, *near, bh, bl)
    _, later[1] = lax.optimization_barrier((top2, later[1]))
    later.append(along_z(later[-1], 1))
    halves = (high, low, far_high, far_low)
    top3, bottom3 = product(3, *halves, bh, bl)
    top1, bottom1 = product(1, *halves, bh, bl)

    top2 = along_reduce(top2, 1)
    bottom2 = along_reduce(bottom2, -1)
    _, later[2] = lax.optimization_barrier((top2, later[2]))
    bottom1 = along_reduce(bottom1, 1)
    top3 = along_reduce(top3, -1)
    top1 = along_reduce(top1 + top2, 1)
    bottom3 = along_reduce(bottom3 + bottom2, -1)
    later.append(along_z(later[-1], 1))
    top0, bottom0 = product(0, *halves, *split_b(later))
    got = swap(bottom0 + bottom1 + bottom3)
    return finish(place, top0, top3, top1, got)


def solution(mesh):
    fine = Mesh(mesh.devices.reshape(N, 2, N, N), ALL)
    return jax.shard_map(
        shards,
        mesh=fine,
        in_specs=(P(ALL, None), P(ALL, None)),
        out_specs=P(("z", "c"), ("y", "x")),
        check_vma=False,
    )
```

```python
import functools
import itertools

import jax
import jax.numpy as jnp
from jax import lax
from jax.experimental import pallas as pl
from jax.experimental.pallas import tpu as pltpu
from jax.sharding import Mesh, PartitionSpec as P

N = 4
ALL = ("z", "c", "y", "x")
VMEM_LIMIT = 16 * 1024 * 1024


def permute(value, target):
    pairs = []
    for z, c, y, x in itertools.product(range(N), range(2), range(N), range(N)):
        tz, tc, ty, tx = target(z, c, y, x)
        place = ((tz % N * 2 + tc % 2) * N + ty % N) * N + tx % N
        pairs.append((((z * 2 + c) * N + y) * N + x, place))
    return lax.ppermute(value, ALL, pairs)


def swap(value):
    return permute(value, lambda z, c, y, x: (z, 1 - c, y, x))


def along_z(value, step):
    return permute(value, lambda z, c, y, x: (z + step * (1 - 2 * c), c, y, x))


def along_gather(value, step):
    return permute(value, lambda z, c, y, x: (z, c, y + step * (1 - c), x + step * c))


def along_reduce(value, step):
    return permute(value, lambda z, c, y, x: (z, c, y + step * c, x + step * (1 - c)))


def split(value):
    high = value.astype(jnp.bfloat16)
    low = (value - high.astype(jnp.float32)).astype(jnp.bfloat16)
    return high, low


def dot(first, second):
    return lax.dot_general(
        first, second, (((1,), (0,)), ((), ())), preferred_element_type=jnp.float32
    )


SMEM = pl.BlockSpec(memory_space=pltpu.SMEM)
VMEM = pl.BlockSpec(memory_space=pltpu.VMEM)
ANY = pl.BlockSpec(memory_space=pl.ANY)
HBM = pl.BlockSpec(memory_space=pltpu.HBM)
PARAMS = pltpu.CompilerParams(vmem_limit_bytes=VMEM_LIMIT)


def prepare_a_kernel(place, a_ref, own_ref, two_ref, side_ref, pass_ref):
    z, c = place[0], place[1]
    half = own_ref.shape[2]

    def piece(step, part):
        start = (lax.rem(z + step, N) * 2 + part) * half
        return a_ref[:, pl.ds(pl.multiple_of(start, half), half)]

    for part in range(2):
        mine = lax.rem(c + part, 2)
        own_ref[part] = piece(0, mine)
        two_ref[part] = piece(2, mine)
        side_ref[part] = piece(1 + 2 * c, mine)
        pass_ref[0, part] = piece(0, 1 - mine)
        pass_ref[1, part] = piece(3 - 2 * c, 1 - mine)


def prepare_a(a, place):
    rows, columns = a.shape
    piece = jax.ShapeDtypeStruct((2, rows, columns // (2 * N)), a.dtype)
    passed = jax.ShapeDtypeStruct((2, 2, rows, columns // (2 * N)), a.dtype)
    return pl.pallas_call(
        prepare_a_kernel,
        out_shape=(piece, piece, piece, passed),
        in_specs=[SMEM, VMEM],
        out_specs=(VMEM,) * 4,
        compiler_params=PARAMS,
        name="prepare_a",
    )(place, a)


AHEAD = 3
ORDER = (2, 3, 1, 0)


def prepare_b_kernel(place, b_ref, keep_ref, pass_ref):
    c, y, x = place[1], place[2], place[3]
    width = keep_ref.shape[2] // N
    for core, ref in ((c, keep_ref), (1 - c, pass_ref)):
        for g in range(N):
            for i, h in enumerate(ORDER):
                ty = lax.rem(y + g * (1 - core) + h * core, N)
                tx = lax.rem(x + g * core + h * (1 - core), N)
                start = pl.multiple_of(((ty * N + tx) * 2 + core) * width, width)
                ref[g, :, i * width : (i + 1) * width] = b_ref[:, pl.ds(start, width)]


def prepare_b(b, place):
    rows, columns = b.shape
    part = jax.ShapeDtypeStruct((N, rows, columns // (2 * N)), b.dtype)
    return pl.pallas_call(
        prepare_b_kernel,
        out_shape=(part, part),
        in_specs=[SMEM, VMEM],
        out_specs=(VMEM, VMEM),
        compiler_params=PARAMS,
        name="prepare_b",
    )(place, b)


def join_a_kernel(side, got, out_ref):
    rows = side.shape[1]
    out_ref[:, :rows] = side[...]
    out_ref[:, rows:] = got[1]


def join_a(side, got):
    _, rows, half = side.shape
    return pl.pallas_call(
        join_a_kernel,
        out_shape=jax.ShapeDtypeStruct((2, 2 * rows, half), side.dtype),
        in_specs=[VMEM] * 2,
        out_specs=VMEM,
        compiler_params=PARAMS,
        name="join_a",
    )(side, got)


def join_b_kernel(keep, got, *refs):
    rows = keep.shape[1]
    for g, ref in enumerate(refs):
        ref[:rows] = keep[g]
        ref[rows:] = got[g]


def join_b(keep, got):
    _, rows, columns = keep.shape
    return pl.pallas_call(
        join_b_kernel,
        out_shape=(jax.ShapeDtypeStruct((2 * rows, columns), keep.dtype),) * N,
        in_specs=[VMEM] * 2,
        out_specs=(VMEM,) * N,
        compiler_params=PARAMS,
        name="join_b",
    )(keep, got)


def panel_kernel(*refs):
    out_refs = refs[N:]
    width = out_refs[0].shape[2]
    for g in range(N):
        out_refs[0][g] = refs[g][:, :width]
        out_refs[1][g] = refs[g][:, width:]


def make_panels(blocks):
    rows, columns = blocks[0].shape
    width = columns * AHEAD // N
    return pl.pallas_call(
        panel_kernel,
        out_shape=(
            jax.ShapeDtypeStruct((N, rows, width), blocks[0].dtype),
            jax.ShapeDtypeStruct((N, rows, columns - width), blocks[0].dtype),
        ),
        in_specs=[VMEM] * N,
        out_specs=(VMEM, VMEM),
        compiler_params=PARAMS,
        name="panel",
    )(*blocks)


def stack_kernel(own, got, side, two, two_got, side_got, *out_refs):
    rows = two.shape[1]
    for part, ref in enumerate(out_refs):
        blocks = [
            own[part],
            got[0, part],
            side[part, :rows],
            side[part, rows:],
            two[part],
            two_got[1 - part],
            side_got[1 - part, rows:],
            side_got[1 - part, :rows],
        ]
        for i, block in enumerate(blocks):
            ref[i * rows : (i + 1) * rows] = block


def stack(own, got, side, two, two_got, side_got):
    _, rows, half = two.shape
    out = jax.ShapeDtypeStruct((2 * N * rows, half), two.dtype)
    return pl.pallas_call(
        stack_kernel,
        out_shape=(out, out),
        in_specs=[VMEM] * 6,
        out_specs=(VMEM, VMEM),
        compiler_params=PARAMS,
        name="stack",
    )(own, got, side, two, two_got, side_got)


NEAR = 3


def split_a_kernel(*refs):
    high_ref, low_ref = refs[2 * NEAR :]
    for i in range(2 * NEAR):
        depth = refs[i].shape[0]
        place = slice(i % NEAR * depth, (i % NEAR + 1) * depth)
        high_ref[i // NEAR, :, place], low_ref[i // NEAR, :, place] = split(refs[i][...].T)


def split_a(tops, bottoms):
    depth, columns = tops[0].shape
    out = jax.ShapeDtypeStruct((2, columns, NEAR * depth), jnp.bfloat16)
    return pl.pallas_call(
        split_a_kernel,
        out_shape=(out, out),
        in_specs=[VMEM] * (2 * NEAR),
        out_specs=(VMEM, VMEM),
        compiler_params=PARAMS,
        name="split_a",
    )(*tops, *bottoms)


def split_b_kernel(*refs):
    high_ref, low_ref = refs[N:]
    slab = refs[0].shape[1]
    for i, g in enumerate((0, 1, 3, 2)):
        for s in range(N):
            place = slice((i * N + s) * slab, (i * N + s + 1) * slab)
            high_ref[place], low_ref[place] = split(refs[s][g])


def split_b(panels):
    _, slab, columns = panels[0].shape
    out = jax.ShapeDtypeStruct((N * N * slab, columns), jnp.bfloat16)
    return pl.pallas_call(
        split_b_kernel,
        out_shape=(out, out),
        in_specs=[VMEM] * N,
        out_specs=(VMEM, VMEM),
        compiler_params=PARAMS,
        name="split_b",
    )(*panels)


TILE = 512


def three_products(high, low, bh, bl):
    return dot(high, bh) + dot(high, bl) + dot(low, bh)


def near_kernel(high, low, bh, bl, *out_refs):
    depth = high.shape[2]
    for half, ref in enumerate(out_refs):
        rows, width = ref.shape
        for start in range(0, rows, TILE):
            tile = slice(start, start + TILE)
            ref[tile] = three_products(
                high[half, tile], low[half, tile], bh[:depth, :width], bl[:depth, :width]
            )


def first_kernel(top, bottom, near_top, near_bottom, bh, bl, far_high, far_low, *out_refs):
    depth = far_high.shape[2]
    rest = slice(bh.shape[0] - depth, bh.shape[0])
    for half, (far, near, ref) in enumerate(zip((top, bottom), (near_top, near_bottom), out_refs)):
        rows, width = ref.shape
        far_high[half], far_low[half] = split(far[...].T)
        for start in range(0, rows, TILE):
            tile = slice(start, start + TILE)
            ref[tile] = near[tile] + three_products(
                far_high[half, tile], far_low[half, tile], bh[rest, :width], bl[rest, :width]
            )


def product_kernel(tasks, high, low, far_high, far_low, bh, bl, *out_refs):
    near = high.shape[2]
    for (half, place), ref in zip(tasks, out_refs):
        rows, width = ref.shape
        columns = slice(place * width, (place + 1) * width)
        for start in range(0, rows, TILE):
            tile = slice(start, start + TILE)
            ref[tile] = three_products(
                high[half, tile], low[half, tile], bh[:near, columns], bl[:near, columns]
            ) + three_products(
                far_high[half, tile], far_low[half, tile], bh[near:, columns], bl[near:, columns]
            )


def cost(rows, depth, width):
    return pl.CostEstimate(
        flops=12 * rows * depth * width, bytes_accessed=8 * rows * width, transcendentals=0
    )


def near_product(high, low, bh, bl):
    _, rows, depth = high.shape
    width = bh.shape[1] // AHEAD
    out = jax.ShapeDtypeStruct((rows, width), jnp.float32)
    return pl.pallas_call(
        near_kernel,
        out_shape=(out, out),
        in_specs=[VMEM] * 4,
        out_specs=(VMEM,) * 2,
        compiler_params=PARAMS,
        cost_estimate=cost(rows, depth, width),
        name="near_product",
    )(high, low, bh, bl)


def first_product(top, bottom, near_top, near_bottom, bh, bl):
    depth, rows = top.shape
    width = bh.shape[1] // AHEAD
    far = jax.ShapeDtypeStruct((2, rows, depth), jnp.bfloat16)
    out = jax.ShapeDtypeStruct((rows, width), jnp.float32)
    return pl.pallas_call(
        first_kernel,
        out_shape=(far, far, out, out),
        in_specs=[VMEM] * 6,
        out_specs=(VMEM,) * 4,
        compiler_params=PARAMS,
        cost_estimate=cost(rows, depth, width),
        name="first_product",
    )(top, bottom, near_top, near_bottom, bh, bl)


def product(r, high, low, far_high, far_low, bh, bl):
    _, rows, depth = far_high.shape
    place = ORDER.index(r)
    width = bh.shape[1] // (AHEAD if place < AHEAD else N - AHEAD)
    out = jax.ShapeDtypeStruct((rows, width), jnp.float32)
    tasks = ((TOP, place % AHEAD), (BOTTOM, place % AHEAD))
    return pl.pallas_call(
        functools.partial(product_kernel, tasks),
        out_shape=(out, out),
        in_specs=[VMEM] * 6,
        out_specs=(VMEM,) * 2,
        compiler_params=PARAMS,
        cost_estimate=cost(rows, N * depth, width),
        name="product",
    )(high, low, far_high, far_low, bh, bl)


def finish_kernel(place, top0, top3, top1, got, out_ref, mine, sems):
    rows, width = top0.shape
    tile = rows // 4
    copies = []
    for k, ref, core in ((1, got, 1 - place[1]), (0, mine, place[1])):
        columns = pl.ds(pl.multiple_of(core * width, width), width)
        for i in range(4):
            tile_rows = slice(i * tile, (i + 1) * tile)
            if k == 0:
                mine[tile_rows] = top0[tile_rows] + top3[tile_rows] + top1[tile_rows]
            copy = pltpu.make_async_copy(
                ref.at[tile_rows], out_ref.at[tile_rows, columns], sems.at[k, i]
            )
            copy.start()
            copies.append(copy)
    for copy in copies:
        copy.wait()


def finish(place, top0, top3, top1, got):
    rows, width = top0.shape
    return pl.pallas_call(
        finish_kernel,
        out_shape=jax.ShapeDtypeStruct((rows, 2 * width), jnp.float32),
        in_specs=[SMEM] + [VMEM] * 4,
        out_specs=HBM,
        scratch_shapes=[pltpu.VMEM((rows, width), jnp.float32), pltpu.SemaphoreType.DMA((2, 4))],
        compiler_params=PARAMS,
        name="finish",
    )(place, top0, top3, top1, got)


TOP, BOTTOM = 0, 1


def shards(a, b):
    place = jnp.stack([lax.axis_index(name) for name in ALL]).astype(jnp.int32)

    own, two, side, handed = prepare_a(a, place)
    two = along_z(two, 2)
    got = swap(handed)
    side = along_z(join_a(side, got), 1)

    keep, give = prepare_b(b, place)
    blocks = join_b(keep, swap(give))
    blocks = [blocks[0]] + [along_gather(blocks[g], g) for g in range(1, N)]
    two, side, blocks = lax.optimization_barrier((two, side, blocks))

    two_got, side_got = swap(two), swap(side)
    panels = make_panels(blocks)
    panels, later = [panels[0]], [panels[1]]
    for _ in range(N - 1):
        panels.append(along_z(panels[-1], 1))
    panels[-1], later[0] = lax.optimization_barrier((panels[-1], later[0]))
    later.append(along_z(later[-1], 1))

    top, bottom = stack(own, got, side, two, two_got, side_got)
    top_behind = along_gather(top, 1)
    bottom_ahead = along_gather(bottom, -1)
    bottom_behind = along_gather(bottom, 1)
    top_ahead = along_gather(top, -1)
    top_far = along_gather(top_behind, 1)
    bottom_far = along_gather(bottom_ahead, -1)

    high, low = split_a((top, top_behind, top_ahead), (bottom, bottom_behind, bottom_ahead))
    bh, bl = split_b(panels)
    near = near_product(high, low, bh, bl)
    far_high, far_low, top2, bottom2 = first_product(top_far, bottom_far, *near, bh, bl)
    _, later[1] = lax.optimization_barrier((top2, later[1]))
    later.append(along_z(later[-1], 1))
    halves = (high, low, far_high, far_low)
    top3, bottom3 = product(3, *halves, bh, bl)
    top1, bottom1 = product(1, *halves, bh, bl)

    top2 = along_reduce(top2, 1)
    bottom2 = along_reduce(bottom2, -1)
    _, later[2] = lax.optimization_barrier((top2, later[2]))
    bottom1 = along_reduce(bottom1, 1)
    top3 = along_reduce(top3, -1)
    top1 = along_reduce(top1 + top2, 1)
    bottom3 = along_reduce(bottom3 + bottom2, -1)
    later.append(along_z(later[-1], 1))
    top0, bottom0 = product(0, *halves, *split_b(later))
    got = swap(bottom0 + bottom1 + bottom3)
    return finish(place, top0, top3, top1, got)


def solution(mesh):
    fine = Mesh(mesh.devices.reshape(N, 2, N, N), ALL)
    return jax.shard_map(
        shards,
        mesh=fine,
        in_specs=(P(ALL, None), P(ALL, None)),
        out_specs=P(("z", "c"), ("y", "x")),
        check_vma=False,
    )
```
